32 devices in a mesh: groups: 2 (over y), sect: 4 (over x, core), tp: 4 (over z).
Axes of the slice: x: 2, y: 2, z: 4, core: 2. Of those that a mesh axis runs over, the one named last changes fastest.
Arguments:
- tokens: bfloat16 [2, 32, 8192], P(None, 'groups', 'tp'), parts along dimension 1, may hold values from -8 to 8, as said below
- gain: bfloat16 [8192], P('tp'), may hold values from 0.25 to 1.75
- w_query: bfloat16 [8192, 8192], P('tp', 'sect'), may hold values from -0.0625 to 0.0625
- w_kv: bfloat16 [8192, 2048], P('tp', 'sect'), may hold values from -0.0625 to 0.0625
- w_out: bfloat16 [8192, 8192], P('sect', 'tp'), may hold values from -0.0625 to 0.0625
- cache: bfloat16 [8, 12288, 2048], P(('groups', 'sect'), 'tp'), parts along dimension 0, may hold values from -122 to 122
- lengths: int32 [8, 4], P(('groups', 'sect')), parts along dimension 0, may hold values from 1 to 8192, as said below
- perm: int32 [32], P('groups'), parts along dimension 0, may hold values from 0 to 15, each once
Outputs:
- mixed: bfloat16 [2, 32, 8192], P(None, 'groups', 'tp'), parts along dimension 1
The draws below stay inside these ranges and needn't reach their ends.
There are 2 independent parts, one for each index of `groups`. The reference program is written for one: setup_inputs(seed, part) draws one part's arguments, and reference() takes and returns one part's arrays. A program takes and returns all parts, laid end to end along the dimension named above; an argument that names none is the same for every part. Nothing has to cross between parts.
Inputs may be any that keep to these rules, and one draw needn't show every extreme that they name: `tokens`: scales vary over the features; features may share an offset across requests and steps. `lengths`: each row sums to 12288; its largest entry is exactly 8192. `perm`: every slot once.
All inputs are finite; a program needn't handle non-finite values.
Results may differ from the reference program's by a relative error of at most 0.0036.
Values may be sent and summed in bfloat16 or wider, within the bound.
A program may use at most 128 MiB of HBM per device.

```python
import math
import jax
import jax.numpy as jnp
from jax import lax

D = 8192
HEADS = 64
KV_HEADS = 8
HEAD_DIM = 128
MAX_LEN = 8192
POOL = 12288
STEPS = 2
REQ_DEV = 4
REQUESTS = 16
N_SECT = 4


def owner_lengths(key):
    key = jax.random.fold_in(key, 5)
    key_order, key_brief, key_share = jax.random.split(key, 3)
    slot_order = jax.vmap(lambda sub_key: jax.random.permutation(sub_key, REQ_DEV))(jax.random.split(key_order, N_SECT)).astype(jnp.int32)
    brief_len = jax.random.randint(key_brief, (N_SECT, 1), 1, 3, dtype=jnp.int32)
    middle_count = REQ_DEV - 2
    remainder = POOL - MAX_LEN - brief_len - middle_count
    shares = jax.random.randint(key_share, (N_SECT, middle_count), 1, 1001, dtype=jnp.int32)
    running = jnp.cumsum(shares, axis=1).astype(jnp.int32)
    limits = (remainder * running // running[:, middle_count - 1:middle_count]).astype(jnp.int32)
    earlier = jnp.concatenate([jnp.zeros((N_SECT, 1), jnp.int32), limits[:, :middle_count - 1]], axis=1)
    middle = (limits - earlier + 1).astype(jnp.int32)
    longest = jnp.full((N_SECT, 1), MAX_LEN, jnp.int32)
    chosen = jnp.concatenate([longest, brief_len, middle], axis=1).astype(jnp.int32)
    row_ids = jnp.arange(N_SECT, dtype=jnp.int32)[:, None]
    return jnp.zeros((N_SECT, REQ_DEV), jnp.int32).at[row_ids, slot_order].set(chosen)


def draw_lengths(key, part):
    return owner_lengths(key)


def draw_tokens(key, part):
    key = jax.random.fold_in(key, 11)
    key_base = jax.random.fold_in(key, 0)
    shape = (STEPS, REQUESTS, D)
    columns = jnp.exp(math.log(3.0) * jnp.arange(D, dtype=jnp.float32) / (D - 1))
    values = jax.random.normal(key_base, shape, jnp.float32) * columns * 0.6
    return jnp.clip(values, -8.0, 8.0).astype(jnp.bfloat16)


def draw_cache(key, part):
    key = jax.random.fold_in(key, 7)
    key_base = jax.random.fold_in(key, 0)
    width = 2 * KV_HEADS * HEAD_DIM
    shape = (N_SECT, POOL, width)
    values = jnp.clip(jax.random.normal(key_base, shape, jnp.float32), -6.0, 6.0)
    return values.astype(jnp.bfloat16)


def levels(own_key, extent, shards, low, high):
    loudness = 1.0
    for dim, parts in shards:
        heights = jax.random.uniform(jax.random.fold_in(jax.random.fold_in(own_key, 6), dim), (parts,), jnp.float32, low / len(shards), high / len(shards))
        loudness = loudness * jnp.repeat(jnp.exp(heights), extent[dim] // parts).reshape((-1,) + (1,) * (len(extent) - 1 - dim))
    return loudness


def normal_values(own_key, dims, deviation, bound, cuts=(), kind=jnp.bfloat16):
    loudness = levels(own_key, dims, cuts, -0.22, 0.18) if cuts else 1.0
    array = jax.random.normal(own_key, dims, jnp.float32) * deviation * loudness
    return jnp.minimum(jnp.maximum(array, -bound), bound).astype(kind)


def setup_inputs(seed: int = 0, part: int = 0) -> dict:
    key_of = jax.random.split(jax.random.key(seed), 9)
    part_keys = jax.random.split(jax.random.fold_in(key_of[8], part), 9)
    return {
        "tokens": draw_tokens(jax.random.fold_in(jax.random.fold_in(key_of[8], part), 71), part),
        "gain": jnp.clip(1.0 + 0.15 * jax.random.normal(key_of[1], (D,), jnp.float32), 0.25, 1.75).astype(jnp.bfloat16),
        "w_query": normal_values(key_of[2], (D, HEADS * HEAD_DIM), D ** -0.5, 0.0625, ((0, 4), (1, 4))),
        "w_kv": normal_values(key_of[3], (D, 2 * KV_HEADS * HEAD_DIM), D ** -0.5, 0.0625, ((0, 4), (1, 4))),
        "w_out": normal_values(key_of[4], (HEADS * HEAD_DIM, D), (HEADS * HEAD_DIM) ** -0.5, 0.0625, ((0, 4), (1, 4))),
        "cache": draw_cache(jax.random.fold_in(jax.random.fold_in(key_of[8], part), 71), part),
        "lengths": draw_lengths(jax.random.fold_in(jax.random.fold_in(key_of[8], part), 71), part),
        "perm": jax.random.permutation(part_keys[7], REQUESTS).astype(jnp.int32),
    }


def rotate(values, places):
    half_dim = values.shape[-1] // 2
    freq_index = jnp.arange(half_dim, dtype=jnp.float32)
    inverse = jnp.exp(-(2.0 * freq_index / values.shape[-1]) * math.log(500000.0))
    angles = places[..., None] * inverse
    cosine = jnp.cos(angles)
    sine = jnp.sin(angles)
    first = values[..., :half_dim]
    second = values[..., half_dim:]
    return jnp.concatenate([first * cosine - second * sine, second * cosine + first * sine], axis=-1)

def attend_owner(operands):
    query_rot, stored, segment, new_keys, new_values = operands
    stored = stored.reshape(POOL, KV_HEADS, 2, HEAD_DIM).astype(jnp.float32)
    key_rows = stored[:, :, 0]
    value_rows = stored[:, :, 1]
    scale = 1.0 / math.sqrt(HEAD_DIM)
    query_full = query_rot.astype(jnp.float32)
    scores = jnp.einsum('jghd,pgd->jghp', query_full, key_rows) * scale
    valid = (segment[None, :] == jnp.arange(REQ_DEV, dtype=jnp.int32)[:, None])[:, None, None, :]
    new_scores = jnp.einsum('jghd,njgd->njgh', query_full, new_keys.astype(jnp.float32)) * scale
    top = jnp.maximum(lax.optimization_barrier(jnp.max(jnp.where(valid, scores, -1e+30), axis=3)), lax.optimization_barrier(jnp.max(new_scores, axis=0)))
    weights = jnp.where(valid, jnp.exp(scores - top[..., None]), 0.0)
    new_weights = jnp.exp(new_scores - top[None])
    total = lax.optimization_barrier(jnp.sum(weights, axis=3)) + lax.optimization_barrier(jnp.sum(new_weights, axis=0))
    weights_low = lax.optimization_barrier(weights.astype(jnp.bfloat16))
    new_low = lax.optimization_barrier(new_weights.astype(jnp.bfloat16))
    blend = jnp.einsum('jghp,pgd->jghd', weights_low.astype(jnp.float32), value_rows)
    blend = blend + jnp.einsum('njgh,njgd->jghd', new_low.astype(jnp.float32), new_values.astype(jnp.float32))
    return (blend / total[..., None]).astype(jnp.bfloat16)

def reference(tokens, gain, w_query, w_kv, w_out, cache, lengths, perm):
    slot_ids = jnp.arange(REQUESTS, dtype=jnp.int32)
    select = (perm[None, :] == slot_ids[:, None]).astype(jnp.bfloat16)
    ends = jnp.cumsum(lengths, axis=1).astype(jnp.int32)
    places = jnp.arange(POOL, dtype=jnp.int32)
    segment = lax.optimization_barrier(jnp.sum((places[None, :, None] >= ends[:, None, :]).astype(jnp.int32), axis=2))
    per_kv = HEADS // KV_HEADS
    earlier_keys = []
    earlier_values = []
    results = []
    for step_index in range(STEPS):
        hidden = tokens[step_index].astype(jnp.float32)
        inv_rms = lax.rsqrt(lax.optimization_barrier(jnp.mean(hidden * hidden, axis=1, keepdims=True)) + 1e-05)
        normed = (hidden * inv_rms * gain.astype(jnp.float32)).astype(jnp.bfloat16)
        query = jnp.dot(normed, w_query, preferred_element_type=jnp.float32).astype(jnp.bfloat16)
        key_value = jnp.dot(normed, w_kv, preferred_element_type=jnp.float32).astype(jnp.bfloat16)
        query_slot = jnp.dot(select, query, preferred_element_type=jnp.float32).astype(jnp.bfloat16)
        query_slot = query_slot.reshape(N_SECT, REQ_DEV, KV_HEADS, per_kv, HEAD_DIM)
        pair_slot = jnp.dot(select, key_value, preferred_element_type=jnp.float32).astype(jnp.bfloat16)
        pair_slot = pair_slot.reshape(N_SECT, REQ_DEV, KV_HEADS, 2, HEAD_DIM)
        positions = (lengths + step_index).astype(jnp.float32)
        query_rot = rotate(query_slot.astype(jnp.float32), positions[:, :, None, None]).astype(jnp.bfloat16)
        new_key = rotate(pair_slot[:, :, :, 0].astype(jnp.float32), positions[:, :, None]).astype(jnp.bfloat16)
        earlier_keys.append(new_key)
        earlier_values.append(pair_slot[:, :, :, 1])
        attended = lax.map(attend_owner, (query_rot, cache, segment, jnp.stack(earlier_keys, axis=1), jnp.stack(earlier_values, axis=1)))
        attended = attended.reshape(REQUESTS, HEADS * HEAD_DIM)
        attn_rows = jnp.dot(select.T, attended, preferred_element_type=jnp.float32).astype(jnp.bfloat16)
        results.append((hidden + jnp.dot(attn_rows, w_out, preferred_element_type=jnp.float32)).astype(jnp.bfloat16))
    return jnp.stack(results)
```

```python
import functools
import math

import jax
import jax.numpy as jnp
import numpy as np
from jax import lax
from jax.experimental import pallas as pl
from jax.experimental.pallas import tpu as pltpu
from jax.sharding import PartitionSpec as P

D = 8192
HEADS = 64
KV_HEADS = 8
HEAD_DIM = 128
PER_KV = HEADS // KV_HEADS
STEPS = 2
LANES = 128
MESH = pl.DeviceIdType.MESH
F32 = jnp.float32
BF16 = jnp.bfloat16


def pack(tiles):
    half = (len(tiles) + 1) // 2
    low = list(tiles[half:])
    if len(low) < half:
        low.append(jnp.zeros_like(tiles[0]))
    top = jnp.concatenate(tiles[:half], axis=1) if half > 1 else tiles[0]
    bottom = jnp.concatenate(low, axis=1) if half > 1 else low[0]
    return jnp.concatenate([top, bottom], axis=0).astype(BF16)


def unpack(packed, count):
    half = (count + 1) // 2
    wide = packed.astype(F32)
    return [
        wide[(i // half) * 8 : (i // half) * 8 + 8, (i % half) * LANES : (i % half + 1) * LANES]
        for i in range(count)
    ]


def kernel(
    cfg,
    perm_ref, len_ref, gain_ref, inv_ref, x_hbm, wq_hbm, wkv_hbm, wo_hbm, cache_hbm,
    out_hbm,
    x_v, wq_v, wkv_v, wo_v, kv_v, bias_v, fin_v, part_v,
    m1, r1, m2, r2, m3, r3, st, rst, m4, r4, m5, r5,
    load_sem, wq_sem, cache_sem, wo_sem,
    s1, e1, s2, e2, s3, e3, s3b, e3b, s4, e4, s5, e5, s6, e6,
):
    n, rows, req, req_dev, block = cfg["n"], cfg["rows"], cfg["req"], cfg["req_dev"], cfg["block"]
    qc, kc = cfg["qc"], cfg["kc"]
    pr, pc, csplit = cfg["pr"], cfg["pc"], cfg["csplit"]
    heads_per = HEADS // n
    total = block + LANES
    s = lax.axis_index("sect")
    t = lax.axis_index("tp")
    same = s == t

    def remote(src, dst, ssem, rsem, sect, tp):
        return pltpu.make_async_remote_copy(
            src_ref=src, dst_ref=dst, send_sem=ssem, recv_sem=rsem,
            device_id={"sect": sect, "tp": tp}, device_id_type=MESH,
        )

    x_copy = pltpu.make_async_copy(x_hbm, x_v, load_sem.at[0])
    x_copy.start()
    nq = cfg["nq"]
    qw = qc // nq
    wq_copies = [
        pltpu.make_async_copy(
            wq_hbm.at[:, pl.ds(i * qw, qw)], wq_v.at[:, pl.ds(i * qw, qw)], wq_sem.at[i]
        )
        for i in range(nq)
    ]
    wkv_copy = pltpu.make_async_copy(wkv_hbm, wkv_v, load_sem.at[1])
    for c in wq_copies:
        c.start()
    wkv_copy.start()
    nc = cfg["nc"]
    cw = block // nc
    cache_copies = [
        pltpu.make_async_copy(
            cache_hbm.at[0, pl.ds(i * cw, cw)], kv_v.at[pl.ds(i * cw, cw)], cache_sem.at[i]
        )
        for i in range(nc)
    ]
    wo_copies = [
        pltpu.make_async_copy(
            wo_hbm.at[:, pl.ds(c * pc, pc)], wo_v.at[:, pl.ds(c * pc, pc)], wo_sem.at[c]
        )
        for c in range(csplit)
    ]

    barrier = pltpu.get_barrier_semaphore()
    for i in range(1, n):
        pl.semaphore_signal(
            barrier, inc=1, device_id={"sect": s, "tp": lax.rem(t + i, n)}, device_id_type=MESH
        )
        pl.semaphore_signal(
            barrier, inc=1, device_id={"sect": lax.rem(s + i, n), "tp": t}, device_id_type=MESH
        )
        pl.semaphore_signal(
            barrier, inc=1, device_id={"sect": lax.rem(s + i, n), "tp": s}, device_id_type=MESH
        )

    @pl.when(jnp.logical_not(same))
    def _():
        pl.semaphore_signal(barrier, inc=1, device_id={"sect": s, "tp": s}, device_id_type=MESH)

    ri = lax.broadcasted_iota(jnp.int32, (rows, rows), 0)
    ci = lax.broadcasted_iota(jnp.int32, (rows, rows), 1)
    big = 4096

    def slot_code(idx):
        return (idx >> 3) * req_dev + (idx & (req_dev - 1)) + ((idx & 7) >= req_dev).astype(jnp.int32) * big

    by_col = jnp.zeros((rows, rows), jnp.int32)
    by_row = jnp.zeros((rows, rows), jnp.int32)
    for c in range(rows):
        code = perm_ref[c % req] + (c // req) * big
        by_col = jnp.where(ci == c, code, by_col)
        by_row = jnp.where(ri == c, code, by_row)
    select = (by_col == slot_code(ri)).astype(F32).astype(BF16)
    select_back = (by_row == slot_code(ci)).astype(F32).astype(BF16)

    x_copy.wait()
    xs = jnp.dot(select, x_v[...], preferred_element_type=F32)
    square = jnp.sum(xs * xs, axis=1, keepdims=True)
    scaled = (xs * gain_ref[...].astype(F32)).astype(BF16)

    r8 = lax.broadcasted_iota(jnp.int32, (8, LANES), 0)
    lane = lax.broadcasted_iota(jnp.int32, (8, LANES), 1)
    lens = [len_ref[0, j] for j in range(req_dev)]
    ends = []
    run = 0
    for j in range(req_dev):
        run = run + lens[j]
        ends.append(run)

    qparts = []
    for i in range(nq):
        wq_copies[i].wait()
        if i < nc:
            cache_copies[i].start()
        qparts.append(
            jnp.dot(scaled, wq_v[:, i * qw : (i + 1) * qw], preferred_element_type=F32)
        )
    for i in range(nq, nc):
        cache_copies[i].start()
    wkv_copy.wait()
    kpart = jnp.dot(scaled, wkv_v[...], preferred_element_type=F32)
    acc = jnp.concatenate(qparts + [kpart], axis=1)
    for c in wo_copies:
        c.start()

    hi = square.astype(BF16).astype(F32)
    lo = square - hi
    lane_r = lax.broadcasted_iota(jnp.int32, (rows, LANES), 1)
    sq_tile = jnp.where(lane_r < 64, hi, lo)
    nt = (qc + kc) // LANES
    for o in range(n):
        sl = slice(o * 8, o * 8 + 8)
        tiles = [acc[sl, i * LANES : (i + 1) * LANES] for i in range(nt)] + [sq_tile[sl]]
        m1[o] = pack(tiles)

    pl.semaphore_wait(barrier, 3 * (n - 1) + jnp.where(same, 0, 1))

    for i in range(1, n):
        to = lax.rem(t + i, n)
        remote(m1.at[to], r1.at[t], s1.at[i], e1.at[t], s, to).start()

    pos = (r8 >= req_dev).astype(jnp.int32)
    step_row = pos
    for j in range(req_dev):
        pos = pos + jnp.where((r8 & (req_dev - 1)) == j, lens[j], 0)
    angle = pos.astype(F32) * inv_ref[...]
    cosine = jnp.cos(angle)
    sine = jnp.sin(angle)
    sine = jnp.where(lane < HEAD_DIM // 2, -sine, sine)
    rj = lax.broadcasted_iota(jnp.int32, (8, total), 0) & (req_dev - 1)
    rk = (lax.broadcasted_iota(jnp.int32, (8, total), 0) >= req_dev).astype(jnp.int32)
    col = lax.broadcasted_iota(jnp.int32, (8, total), 1)
    first = t * block
    low_b = jnp.zeros((8, total), jnp.int32)
    high_b = jnp.zeros((8, total), jnp.int32)
    for j in range(req_dev):
        low_b = jnp.where(rj == j, ends[j] - lens[j] - first, low_b)
        high_b = jnp.where(rj == j, ends[j] - first, high_b)
    old_ok = (col >= low_b) & (col < high_b) & (col < block)
    nidx = col - block
    new_limit = jnp.where(t == 0, block + 8, block)
    new_ok = (
        (col >= block) & (col < new_limit) & ((nidx & (req_dev - 1)) == rj)
        & ((nidx >= req_dev).astype(jnp.int32) <= rk)
    )
    bias_v[...] = jnp.where(old_ok | new_ok, 0.0, -1e30)
    kv_v[block + 16 : total, :] = jnp.zeros((LANES - 16, 2 * KV_HEADS * HEAD_DIM), BF16)

    sums = unpack(m1[t], nt + 1)
    for i in range(1, n):
        src = lax.rem(t + i, n)
        remote(m1.at[src], r1.at[src], s1.at[i], e1.at[src], s, src).wait_recv()
        sums = [a + b for a, b in zip(sums, unpack(r1[src], nt + 1))]
    sq = sums[nt][:, 0:1] + sums[nt][:, 64:65]
    inv_rms = lax.rsqrt(sq * (1.0 / D) + 1e-05)
    m2[...] = pack([a * inv_rms for a in sums[:nt]])

    for i in range(1, n):
        to = lax.rem(t + i, n)
        remote(m2, r2.at[s], s2.at[i], e2.at[s], t, to).start()

    @pl.when(jnp.logical_not(same))
    def _():
        remote(m2, r2.at[s], s2.at[0], e2.at[s], t, t).start()

    @pl.when(same)
    def _():
        r2[s] = m2[...]

    for c in cache_copies:
        c.wait()
    for src in range(n):
        @pl.when(jnp.logical_not(same & (s == src)))
        def _():
            remote(m2, r2.at[src], s2.at[0], e2.at[src], t, t).wait_recv()

    tiles = [unpack(r2[src], nt) for src in range(n)]
    qt = qc // LANES
    kt = kc // LANES

    def q_tile(head):
        return tiles[head // qt][head % qt]

    def kv_tile(index):
        return tiles[index // kt][qt + index % kt]

    def rotate(a):
        return a * cosine + pltpu.roll(a, HEAD_DIM // 2, 1) * sine

    factor = math.log2(math.e) / math.sqrt(HEAD_DIM)
    blends = []
    tops = []
    totals = []
    sent = 0
    zero8 = jnp.zeros((8, LANES), F32)
    for g in range(KV_HEADS):
        kcol = slice(g * 256, g * 256 + 128)
        vcol = slice(g * 256 + 128, g * 256 + 256)
        kv_v[block : block + 16, kcol] = jnp.concatenate(
            [rotate(kv_tile(2 * g)), zero8], axis=0
        ).astype(BF16)
        kv_v[block : block + 16, vcol] = jnp.concatenate(
            [kv_tile(2 * g + 1), zero8], axis=0
        ).astype(BF16)
        q = jnp.concatenate(
            [rotate(q_tile(g * PER_KV + h)) for h in range(PER_KV)], axis=0
        ).astype(BF16)
        sc = lax.dot_general(
            q, kv_v[:, kcol], (((1,), (1,)), ((), ())), preferred_element_type=F32
        )
        sc = sc.reshape(PER_KV, 8, total) * factor + bias_v[...][None]
        top = jnp.maximum(jnp.max(sc, axis=2, keepdims=True), -1e20)
        w = jnp.exp2(sc - top)
        tot = jnp.sum(w, axis=2, keepdims=True)
        o = jnp.dot(
            w.reshape(PER_KV * 8, total).astype(BF16), kv_v[:, vcol],
            preferred_element_type=F32,
        )
        for h in range(PER_KV):
            blends.append(o[h * 8 : h * 8 + 8])
            tops.append(top[h])
            totals.append(tot[h])
        while (sent + 1) * heads_per <= len(blends):
            d = sent
            hs = range(d * heads_per, (d + 1) * heads_per)
            m3[d] = pack([blends[h] for h in hs])
            stat = zero8
            for a, h in enumerate(hs):
                stat = jnp.where(lane == a, tops[h], stat)
                stat = jnp.where(lane == 64 + a, totals[h], stat)
            st[d] = stat

            @pl.when(t != d)
            def _():
                remote(st.at[d], rst.at[t], s3b.at[d], e3b.at[t], s, d).start()
                remote(m3.at[d], r3.at[t], s3.at[d], e3.at[t], s, d).start()

            sent += 1

    stats = [st[t]]
    for i in range(1, n):
        src = lax.rem(t + i, n)
        remote(st.at[src], rst.at[src], s3b.at[src], e3b.at[src], s, src).wait_recv()
        stats.append(rst[src])
    best = functools.reduce(jnp.maximum, stats)
    decay = [jnp.exp2(jnp.minimum(a - best, 0.0)) for a in stats]
    norm = sum(f * pltpu.roll(a, 64, 1) for f, a in zip(decay, stats))
    share = [f / norm for f in decay]
    att = [a * share[0][:, i : i + 1] for i, a in enumerate(unpack(m3[t], heads_per))]
    for i in range(1, n):
        src = lax.rem(t + i, n)
        remote(m3.at[src], r3.at[src], s3.at[src], e3.at[src], s, src).wait_recv()
        att = [
            a + b * share[i][:, k : k + 1]
            for k, (a, b) in enumerate(zip(att, unpack(r3[src], heads_per)))
        ]
    m4[...] = pack(att)

    for i in range(1, n):
        to = lax.rem(t + i, n)
        remote(m4, r4.at[s], s4.at[i], e4.at[s], t, to).start()

    @pl.when(jnp.logical_not(same))
    def _():
        remote(m4, r4.at[s], s4.at[0], e4.at[s], t, t).start()

    @pl.when(same)
    def _():
        r4[s] = m4[...]

    for src in range(n):
        @pl.when(jnp.logical_not(same & (s == src)))
        def _():
            remote(m4, r4.at[src], s4.at[0], e4.at[src], t, t).wait_recv()

    attended = jnp.concatenate(
        [jnp.concatenate(unpack(r4[src], heads_per), axis=1) for src in range(n)], axis=0
    ).astype(BF16)
    attended = jnp.dot(select_back, attended, preferred_element_type=F32).astype(BF16)

    for c in range(csplit):
        wo_copies[c].wait()
        part = jnp.dot(attended, wo_v[:, c * pc : (c + 1) * pc], preferred_element_type=F32)
        for r in range(n // csplit):
            p = r * csplit + c
            piece = part[r * pr : (r + 1) * pr]
            part_v[p] = piece
            m5[p] = piece.astype(BF16)

            @pl.when(s != p)
            def _():
                remote(m5.at[p], r5.at[s], s5.at[p], e5.at[s], p, t).start()

    prow = pl.ds(pl.multiple_of((s // csplit) * pr, pr), pr)
    pcol = pl.ds(pl.multiple_of(lax.rem(s, csplit) * pc, pc), pc)
    result = part_v[s] + x_v[prow, pcol].astype(F32)
    for i in range(1, n):
        src = lax.rem(s + i, n)
        remote(m5.at[src], r5.at[src], s5.at[src], e5.at[src], src, t).wait_recv()
        result = result + r5[src].astype(F32)
    fin_v[...] = result.astype(BF16)
    mine = out_hbm.at[prow, pcol]
    for i in range(1, n):
        remote(fin_v, mine, s6.at[i], e6.at[s], lax.rem(s + i, n), t).start()
    own = pltpu.make_async_copy(fin_v, mine, load_sem.at[2])
    own.start()

    for i in range(1, n):
        to = lax.rem(t + i, n)
        remote(m1.at[to], r1.at[t], s1.at[i], e1.at[t], s, to).wait_send()
        remote(m2, r2.at[s], s2.at[i], e2.at[s], t, to).wait_send()
        remote(m4, r4.at[s], s4.at[i], e4.at[s], t, to).wait_send()
        remote(m3.at[to], r3.at[t], s3.at[to], e3.at[t], s, to).wait_send()
        remote(st.at[to], rst.at[t], s3b.at[to], e3b.at[t], s, to).wait_send()
        across = lax.rem(s + i, n)
        remote(m5.at[across], r5.at[s], s5.at[across], e5.at[s], across, t).wait_send()

    @pl.when(jnp.logical_not(same))
    def _():
        remote(m2, r2.at[s], s2.at[0], e2.at[s], t, t).wait_send()
        remote(m4, r4.at[s], s4.at[0], e4.at[s], t, t).wait_send()

    own.wait()
    for i in range(1, n):
        src = lax.rem(s + i, n)
        srow = pl.ds(pl.multiple_of((src // csplit) * pr, pr), pr)
        scol = pl.ds(pl.multiple_of(lax.rem(src, csplit) * pc, pc), pc)
        remote(fin_v, mine, s6.at[i], e6.at[s], src, t).wait_send()
        remote(fin_v, out_hbm.at[srow, scol], s6.at[i], e6.at[src], src, t).wait_recv()


def per_device(n, tokens, gain, w_query, w_kv, w_out, cache, lengths, perm):
    steps, req, feat = tokens.shape
    rows = steps * req
    req_dev = lengths.shape[1]
    block = cache.shape[1]
    qc, kc = w_query.shape[1], w_kv.shape[1]
    cols = w_out.shape[1]
    csplit = min(n, cols // LANES)
    pr, pc = rows // (n // csplit), cols // csplit
    heads_per = HEADS // n
    nt = (qc + kc) // LANES
    assert steps == STEPS and steps * req_dev == 8 and req == n * req_dev
    cfg = dict(
        n=n, rows=rows, req=req, req_dev=req_dev, block=block, qc=qc, kc=kc,
        csplit=csplit, pr=pr, pc=pc, nq=max(1, qc // 512), nc=4,
    )
    w1 = (nt + 2) // 2 * LANES
    w2 = (nt + 1) // 2 * LANES
    w3 = (heads_per + 1) // 2 * LANES
    inv = np.exp(-(2.0 * np.arange(64) / HEAD_DIM) * math.log(500000.0)).astype(np.float32)
    inv = jnp.asarray(np.concatenate([inv, inv])[None])
    any_spec = pl.BlockSpec(memory_space=pl.ANY)
    smem = pl.BlockSpec(memory_space=pltpu.SMEM)
    vmem = pl.BlockSpec(memory_space=pltpu.VMEM)
    dma = pltpu.SemaphoreType.DMA
    out = pl.pallas_call(
        functools.partial(kernel, cfg),
        out_shape=jax.ShapeDtypeStruct((rows, cols), BF16),
        in_specs=[smem, smem, vmem, vmem] + [any_spec] * 5,
        out_specs=any_spec,
        scratch_shapes=[
            pltpu.VMEM((rows, feat), BF16),
            pltpu.VMEM(w_query.shape, BF16),
            pltpu.VMEM(w_kv.shape, BF16),
            pltpu.VMEM(w_out.shape, BF16),
            pltpu.VMEM((block + LANES, cache.shape[2]), BF16),
            pltpu.VMEM((8, block + LANES), F32),
            pltpu.VMEM((pr, pc), BF16),
            pltpu.VMEM((n, pr, pc), F32),
            pltpu.VMEM((n, 16, w1), BF16),
            pltpu.VMEM((n, 16, w1), BF16),
            pltpu.VMEM((16, w2), BF16),
            pltpu.VMEM((n, 16, w2), BF16),
            pltpu.VMEM((n, 16, w3), BF16),
            pltpu.VMEM((n, 16, w3), BF16),
            pltpu.VMEM((n, 8, LANES), F32),
            pltpu.VMEM((n, 8, LANES), F32),
            pltpu.VMEM((16, w3), BF16),
            pltpu.VMEM((n, 16, w3), BF16),
            pltpu.VMEM((n, pr, pc), BF16),
            pltpu.VMEM((n, pr, pc), BF16),
            dma((3,)),
            dma((cfg["nq"],)),
            dma((cfg["nc"],)),
            dma((csplit,)),
        ]
        + [dma((n,)) for _ in range(14)],
        compiler_params=pltpu.CompilerParams(
            collective_id=0, has_side_effects=True, vmem_limit_bytes=56 * 1024 * 1024
        ),
        cost_estimate=pl.CostEstimate(
            flops=2 * rows * feat * (qc + kc + cols) + 4 * 64 * block * 8 * 128,
            bytes_accessed=2 * (feat * (qc + kc) + w_out.size + cache.size),
            transcendentals=64 * 8 * block,
        ),
    )(
        perm, lengths, gain.reshape(1, feat), inv,
        tokens.reshape(rows, feat), w_query, w_kv, w_out, cache,
    )
    return out.reshape(steps, req, cols)


def solution(mesh):
    n = mesh.shape["sect"]
    assert mesh.shape["tp"] == n
    return jax.shard_map(
        functools.partial(per_device, n),
        mesh=mesh,
        in_specs=(
            P(None, "groups", "tp"),
            P("tp"),
            P("tp", "sect"),
            P("tp", "sect"),
            P("sect", "tp"),
            P(("groups", "sect"), "tp", None),
            P(("groups", "sect"), None),
            P("groups"),
        ),
        out_specs=P(None, "groups", "tp"),
        check_vma=False,
    )
```

```python
import functools
import math

import jax
import jax.numpy as jnp
import numpy as np
from jax import lax
from jax.experimental import pallas as pl
from jax.experimental.pallas import tpu as pltpu
from jax.sharding import PartitionSpec as P

D = 8192
HEADS = 64
KV_HEADS = 8
HEAD_DIM = 128
PER_KV = HEADS // KV_HEADS
STEPS = 2
LANES = 128
MESH = pl.DeviceIdType.MESH
F32 = jnp.float32
BF16 = jnp.bfloat16


def pack(tiles):
    half = (len(tiles) + 1) // 2
    low = list(tiles[half:])
    if len(low) < half:
        low.append(jnp.zeros_like(tiles[0]))
    top = jnp.concatenate(tiles[:half], axis=1) if half > 1 else tiles[0]
    bottom = jnp.concatenate(low, axis=1) if half > 1 else low[0]
    return jnp.concatenate([top, bottom], axis=0).astype(BF16)


def unpack(packed, count):
    half = (count + 1) // 2
    wide = packed.astype(F32)
    return [
        wide[(i // half) * 8 : (i // half) * 8 + 8, (i % half) * LANES : (i % half + 1) * LANES]
        for i in range(count)
    ]


def kernel(
    cfg,
    perm_ref, len_ref, gain_ref, inv_ref, x_hbm, wq_hbm, wkv_hbm, wo_hbm, cache_hbm,
    out_hbm,
    x_v, wq_v, wkv_v, wo_v, kv_v, bias_v, fin_v,
    m1, r1, m2, r2, m3, r3, st, rst, m4, r4, m5, r5,
    load_sem, wq_sem, cache_sem, wo_sem, out_sem,
    s1, e1, s2, e2, s3, e3, s3b, e3b, s4, e4, s5, e5,
):
    n, rows, req, req_dev, block = cfg["n"], cfg["rows"], cfg["req"], cfg["req_dev"], cfg["block"]
    qc, kc, nq, unit, nu = cfg["qc"], cfg["kc"], cfg["nq"], cfg["unit"], cfg["nu"]
    nch, cw = cfg["nch"], cfg["cw"]
    heads_per = HEADS // n
    total = block + LANES
    s = lax.axis_index("sect")
    t = lax.axis_index("tp")
    same = s == t

    def remote(src, dst, ssem, rsem, sect, tp):
        return pltpu.make_async_remote_copy(
            src_ref=src, dst_ref=dst, send_sem=ssem, recv_sem=rsem,
            device_id={"sect": sect, "tp": tp}, device_id_type=MESH,
        )

    x_copy = pltpu.make_async_copy(x_hbm, x_v, load_sem.at[0])
    x_copy.start()
    wkv_copy = pltpu.make_async_copy(wkv_hbm, wkv_v, load_sem.at[1])
    wkv_copy.start()
    qw = qc // nq
    wq_copies = [
        pltpu.make_async_copy(
            wq_hbm.at[:, pl.ds(i * qw, qw)], wq_v.at[:, pl.ds(i * qw, qw)], wq_sem.at[i]
        )
        for i in range(nq)
    ]
    for c in wq_copies:
        c.start()
    nc = cfg["nc"]
    crows = block // nc
    cache_copies = [
        pltpu.make_async_copy(
            cache_hbm.at[0, pl.ds(i * crows, crows)],
            kv_v.at[pl.ds(i * crows, crows)],
            cache_sem.at[i],
        )
        for i in range(nc)
    ]
    uw = unit * HEAD_DIM
    wo_copies = [
        pltpu.make_async_copy(wo_hbm.at[pl.ds(u * uw, uw)], wo_v.at[pl.ds(u * uw, uw)], wo_sem.at[u])
        for u in range(nu)
    ]

    barrier = pltpu.get_barrier_semaphore()
    for i in range(1, n):
        pl.semaphore_signal(
            barrier, inc=1, device_id={"sect": s, "tp": lax.rem(t + i, n)}, device_id_type=MESH
        )
        pl.semaphore_signal(
            barrier, inc=1, device_id={"sect": lax.rem(s + i, n), "tp": t}, device_id_type=MESH
        )
        pl.semaphore_signal(
            barrier, inc=1, device_id={"sect": lax.rem(s + i, n), "tp": s}, device_id_type=MESH
        )

    @pl.when(jnp.logical_not(same))
    def _():
        pl.semaphore_signal(barrier, inc=1, device_id={"sect": s, "tp": s}, device_id_type=MESH)

    ri = lax.broadcasted_iota(jnp.int32, (rows, rows), 0)
    ci = lax.broadcasted_iota(jnp.int32, (rows, rows), 1)
    big = 4096

    def slot_code(idx):
        return (idx >> 3) * req_dev + (idx & (req_dev - 1)) + ((idx & 7) >= req_dev).astype(jnp.int32) * big

    by_col = jnp.zeros((rows, rows), jnp.int32)
    by_row = jnp.zeros((rows, rows), jnp.int32)
    for c in range(rows):
        code = perm_ref[c % req] + (c // req) * big
        by_col = jnp.where(ci == c, code, by_col)
        by_row = jnp.where(ri == c, code, by_row)
    select = (by_col == slot_code(ri)).astype(F32).astype(BF16)
    select_back = (by_row == slot_code(ci)).astype(F32).astype(BF16)

    x_copy.wait()
    xs = jnp.dot(select, x_v[...], preferred_element_type=F32)
    square = jnp.sum(xs * xs, axis=1, keepdims=True)
    scaled = (xs * gain_ref[...].astype(F32).reshape(1, -1)).astype(BF16)

    r8 = lax.broadcasted_iota(jnp.int32, (8, LANES), 0)
    lane = lax.broadcasted_iota(jnp.int32, (8, LANES), 1)
    lens = [len_ref[0, j] for j in range(req_dev)]
    ends = []
    run = 0
    for j in range(req_dev):
        run = run + lens[j]
        ends.append(run)

    hi = square.astype(BF16).astype(F32)
    lo = square - hi
    lane_r = lax.broadcasted_iota(jnp.int32, (rows, LANES), 1)
    sq_tile = jnp.where(lane_r < 64, hi, lo)
    qt = qw // LANES
    kt = kc // LANES
    counts = [qt + (kt if h == 0 else 0) for h in range(nq)]
    w1 = [pl.ds(0, (counts[h] + (h == 0) + 1) // 2 * LANES) for h in range(nq)]
    w2 = [pl.ds(0, (counts[h] + 1) // 2 * LANES) for h in range(nq)]

    def tile_rows(array, o):
        return [
            array[o * 8 : o * 8 + 8, i * LANES : (i + 1) * LANES]
            for i in range(array.shape[1] // LANES)
        ]

    wkv_copy.wait()
    kpart = jnp.dot(scaled, wkv_v[...], preferred_element_type=F32)
    for h in range(nq):
        wq_copies[h].wait()
        if h == nq - 1:
            for c in cache_copies:
                c.start()
            for c in wo_copies:
                c.start()
        qpart = jnp.dot(scaled, wq_v[:, h * qw : (h + 1) * qw], preferred_element_type=F32)
        for o in range(n):
            tiles = tile_rows(qpart, o)
            if h == 0:
                tiles = tile_rows(kpart, o) + tiles + [sq_tile[o * 8 : o * 8 + 8]]
            m1[h, o, :, w1[h]] = pack(tiles)
        if h == 0:
            pl.semaphore_wait(barrier, 3 * (n - 1) + jnp.where(same, 0, 1))
        for i in range(1, n):
            to = lax.rem(t + i, n)
            remote(
                m1.at[h, to, :, w1[h]], r1.at[h, t, :, w1[h]], s1.at[h, i], e1.at[h, t], s, to
            ).start()

    pos = (r8 >= req_dev).astype(jnp.int32)
    step_row = pos
    for j in range(req_dev):
        pos = pos + jnp.where((r8 & (req_dev - 1)) == j, lens[j], 0)
    angle = pos.astype(F32) * inv_ref[...]
    cosine = jnp.cos(angle)
    sine = jnp.sin(angle)
    sine = jnp.where(lane < HEAD_DIM // 2, -sine, sine)
    rj = lax.broadcasted_iota(jnp.int32, (8, total), 0) & (req_dev - 1)
    rk = (lax.broadcasted_iota(jnp.int32, (8, total), 0) >= req_dev).astype(jnp.int32)
    col = lax.broadcasted_iota(jnp.int32, (8, total), 1)
    first = t * block
    low_b = jnp.zeros((8, total), jnp.int32)
    high_b = jnp.zeros((8, total), jnp.int32)
    for j in range(req_dev):
        low_b = jnp.where(rj == j, ends[j] - lens[j] - first, low_b)
        high_b = jnp.where(rj == j, ends[j] - first, high_b)
    old_ok = (col >= low_b) & (col < high_b) & (col < block)
    nidx = col - block
    new_limit = jnp.where(t == 0, block + 8, block)
    new_ok = (
        (col >= block) & (col < new_limit) & ((nidx & (req_dev - 1)) == rj)
        & ((nidx >= req_dev).astype(jnp.int32) <= rk)
    )
    bias_v[...] = jnp.where(old_ok | new_ok, 0.0, -1e30)
    kv_v[block + 16 : total, :] = jnp.zeros((LANES - 16, 2 * KV_HEADS * HEAD_DIM), BF16)

    inv_rms = None
    for h in range(nq):
        count = counts[h] + (h == 0)
        sums = unpack(m1[h, t, :, w1[h]], count)
        for i in range(1, n):
            src = lax.rem(t + i, n)
            remote(
                m1.at[h, src, :, w1[h]], r1.at[h, src, :, w1[h]], s1.at[h, i], e1.at[h, src], s, src
            ).wait_recv()
            sums = [a + b for a, b in zip(sums, unpack(r1[h, src, :, w1[h]], count))]
        if h == 0:
            sq = sums[-1][:, 0:1] + sums[-1][:, 64:65]
            inv_rms = lax.rsqrt(sq * (1.0 / D) + 1e-05)
            sums = sums[:-1]
        m2[h, :, w2[h]] = pack([a * inv_rms for a in sums])
        for i in range(1, n):
            to = lax.rem(t + i, n)
            remote(
                m2.at[h, :, w2[h]], r2.at[h, s, :, w2[h]], s2.at[h, i], e2.at[h, s], t, to
            ).start()

        @pl.when(jnp.logical_not(same))
        def _():
            remote(
                m2.at[h, :, w2[h]], r2.at[h, s, :, w2[h]], s2.at[h, 0], e2.at[h, s], t, t
            ).start()

        @pl.when(same)
        def _():
            r2[h, s, :, w2[h]] = m2[h, :, w2[h]]

    for c in cache_copies:
        c.wait()
    held = {}

    def routed(src, h):
        if (src, h) not in held:
            @pl.when(jnp.logical_not(same & (s == src)))
            def _():
                remote(
                    m2.at[h, :, w2[h]], r2.at[h, src, :, w2[h]], s2.at[h, 0], e2.at[h, src], t, t
                ).wait_recv()

            held[src, h] = unpack(r2[h, src, :, w2[h]], counts[h])
        return held[src, h]

    per_src = nq * qt

    def q_tile(head):
        src, inner = head // per_src, head % per_src
        return routed(src, inner // qt)[(kt if inner // qt == 0 else 0) + inner % qt]

    def kv_tile(index):
        return routed(index // kt, 0)[index % kt]

    def rotate(a):
        return a * cosine + pltpu.roll(a, HEAD_DIM // 2, 1) * sine

    def last_part(g):
        return max((head % per_src) // qt for head in range(g * PER_KV, (g + 1) * PER_KV))

    factor = math.log2(math.e) / math.sqrt(HEAD_DIM)
    zero8 = jnp.zeros((8, LANES), F32)
    for g in sorted(range(KV_HEADS), key=lambda g: (last_part(g), g)):
        kcol = slice(g * 256, g * 256 + 128)
        vcol = slice(g * 256 + 128, g * 256 + 256)
        kv_v[block : block + 16, kcol] = jnp.concatenate(
            [rotate(kv_tile(2 * g)), zero8], axis=0
        ).astype(BF16)
        kv_v[block : block + 16, vcol] = jnp.concatenate(
            [kv_tile(2 * g + 1), zero8], axis=0
        ).astype(BF16)
        q = jnp.concatenate(
            [rotate(q_tile(g * PER_KV + h)) for h in range(PER_KV)], axis=0
        ).astype(BF16)
        sc = lax.dot_general(
            q, kv_v[:, kcol], (((1,), (1,)), ((), ())), preferred_element_type=F32
        )
        sc = sc.reshape(PER_KV, 8, total) * factor + bias_v[...][None]
        top = jnp.maximum(jnp.max(sc, axis=2, keepdims=True), -1e20)
        w = jnp.exp2(sc - top)
        tot = jnp.sum(w, axis=2, keepdims=True)
        o = jnp.dot(
            w.reshape(PER_KV * 8, total).astype(BF16), kv_v[:, vcol],
            preferred_element_type=F32,
        )
        for first_head in range(0, PER_KV, unit):
            head = g * PER_KV + first_head
            d, u = head // heads_per, (head % heads_per) // unit
            hs = range(first_head, first_head + unit)
            m3[u, d] = pack([o[h * 8 : h * 8 + 8] for h in hs])
            stat = zero8
            for a, h in enumerate(hs):
                stat = jnp.where(lane == a, top[h], stat)
                stat = jnp.where(lane == 64 + a, tot[h], stat)
            st[u, d] = stat

            @pl.when(t != d)
            def _():
                remote(st.at[u, d], rst.at[u, t], s3b.at[u, d], e3b.at[u, t], s, d).start()
                remote(m3.at[u, d], r3.at[u, t], s3.at[u, d], e3.at[u, t], s, d).start()

    for u in range(nu):
        stats = [st[u, t]]
        for i in range(1, n):
            src = lax.rem(t + i, n)
            remote(
                st.at[u, src], rst.at[u, src], s3b.at[u, src], e3b.at[u, src], s, src
            ).wait_recv()
            stats.append(rst[u, src])
        best = functools.reduce(jnp.maximum, stats)
        decay = [jnp.exp2(jnp.minimum(a - best, 0.0)) for a in stats]
        norm = sum(f * pltpu.roll(a, 64, 1) for f, a in zip(decay, stats))
        share = [f / norm for f in decay]
        att = [a * share[0][:, i : i + 1] for i, a in enumerate(unpack(m3[u, t], unit))]
        for i in range(1, n):
            src = lax.rem(t + i, n)
            remote(m3.at[u, src], r3.at[u, src], s3.at[u, src], e3.at[u, src], s, src).wait_recv()
            att = [
                a + b * share[i][:, k : k + 1]
                for k, (a, b) in enumerate(zip(att, unpack(r3[u, src], unit)))
            ]
        m4[u] = pack(att)
        for i in range(1, n):
            to = lax.rem(t + i, n)
            remote(m4.at[u], r4.at[u, s], s4.at[u, i], e4.at[u, s], t, to).start()

        @pl.when(jnp.logical_not(same))
        def _():
            remote(m4.at[u], r4.at[u, s], s4.at[u, 0], e4.at[u, s], t, t).start()

        @pl.when(same)
        def _():
            r4[u, s] = m4[u]

    lefts = []
    for u in range(nu):
        for src in range(n):
            @pl.when(jnp.logical_not(same & (s == src)))
            def _():
                remote(m4.at[u], r4.at[u, src], s4.at[u, 0], e4.at[u, src], t, t).wait_recv()

        attended = jnp.concatenate(
            [jnp.concatenate(unpack(r4[u, src], unit), axis=1) for src in range(n)], axis=0
        ).astype(BF16)
        lefts.append(jnp.dot(select_back, attended, preferred_element_type=F32).astype(BF16))
        wo_copies[u].wait()
        if u < nu - 1:
            early = jnp.dot(lefts[u], wo_v[u * uw : (u + 1) * uw, :], preferred_element_type=F32)
            fin_v[...] = early if u == 0 else fin_v[...] + early

    u = nu - 1
    for c in range(nch):
        ccol = slice(c * cw, (c + 1) * cw)
        part = jnp.dot(lefts[u], wo_v[u * uw : (u + 1) * uw, ccol], preferred_element_type=F32)
        if nu > 1:
            part = part + fin_v[:, ccol]
        m5[c] = part.astype(BF16)
        for i in range(1, n):
            to = lax.rem(s + i, n)
            remote(m5.at[c], r5.at[c, s], s5.at[c, i], e5.at[c, s], to, t).start()
        r5[c, s] = m5[c]

    for i in range(1, n):
        to = lax.rem(t + i, n)
        for h in range(nq):
            remote(
                m1.at[h, to, :, w1[h]], r1.at[h, t, :, w1[h]], s1.at[h, i], e1.at[h, t], s, to
            ).wait_send()
            remote(
                m2.at[h, :, w2[h]], r2.at[h, s, :, w2[h]], s2.at[h, i], e2.at[h, s], t, to
            ).wait_send()
        for u in range(nu):
            remote(m4.at[u], r4.at[u, s], s4.at[u, i], e4.at[u, s], t, to).wait_send()
            remote(m3.at[u, to], r3.at[u, t], s3.at[u, to], e3.at[u, t], s, to).wait_send()
            remote(st.at[u, to], rst.at[u, t], s3b.at[u, to], e3b.at[u, t], s, to).wait_send()

    @pl.when(jnp.logical_not(same))
    def _():
        for h in range(nq):
            remote(
                m2.at[h, :, w2[h]], r2.at[h, s, :, w2[h]], s2.at[h, 0], e2.at[h, s], t, t
            ).wait_send()
        for u in range(nu):
            remote(m4.at[u], r4.at[u, s], s4.at[u, 0], e4.at[u, s], t, t).wait_send()

    outs = []
    for c in range(nch):
        ccol = slice(c * cw, (c + 1) * cw)
        for i in range(1, n):
            src = lax.rem(s + i, n)
            remote(m5.at[c], r5.at[c, src], s5.at[c, i], e5.at[c, src], src, t).wait_recv()
        result = x_v[:, ccol].astype(F32)
        for src in range(n):
            result = result + r5[c, src].astype(F32)
        x_v[:, ccol] = result.astype(BF16)
        outs.append(
            pltpu.make_async_copy(x_v.at[:, ccol], out_hbm.at[:, ccol], out_sem.at[c])
        )
        outs[c].start()
    for c in range(nch):
        for i in range(1, n):
            to = lax.rem(s + i, n)
            remote(m5.at[c], r5.at[c, s], s5.at[c, i], e5.at[c, s], to, t).wait_send()
        outs[c].wait()


def per_device(n, tokens, gain, w_query, w_kv, w_out, cache, lengths, perm):
    steps, req, feat = tokens.shape
    rows = steps * req
    req_dev = lengths.shape[1]
    block = cache.shape[1]
    qc, kc = w_query.shape[1], w_kv.shape[1]
    cols = w_out.shape[1]
    heads_per = HEADS // n
    unit = min(heads_per, PER_KV)
    nu = heads_per // unit
    nq = max(1, qc // 1024)
    nch = max(1, cols // 1024)
    cw = cols // nch
    assert steps == STEPS and steps * req_dev == 8 and req == n * req_dev
    cfg = dict(
        n=n, rows=rows, req=req, req_dev=req_dev, block=block, qc=qc, kc=kc,
        nq=nq, nc=4, unit=unit, nu=nu, nch=nch, cw=cw,
    )
    widest = qc // nq // LANES + kc // LANES
    w1 = (widest + 2) // 2 * LANES
    w2 = (widest + 1) // 2 * LANES
    w3 = (unit + 1) // 2 * LANES
    inv = np.exp(-(2.0 * np.arange(64) / HEAD_DIM) * math.log(500000.0)).astype(np.float32)
    inv = jnp.asarray(np.concatenate([inv, inv])[None])
    any_spec = pl.BlockSpec(memory_space=pl.ANY)
    smem = pl.BlockSpec(memory_space=pltpu.SMEM)
    vmem = pl.BlockSpec(memory_space=pltpu.VMEM)
    dma = pltpu.SemaphoreType.DMA
    out = pl.pallas_call(
        functools.partial(kernel, cfg),
        out_shape=jax.ShapeDtypeStruct((rows, cols), BF16),
        in_specs=[smem, smem, vmem, vmem] + [any_spec] * 5,
        out_specs=any_spec,
        scratch_shapes=[
            pltpu.VMEM((rows, feat), BF16),
            pltpu.VMEM(w_query.shape, BF16),
            pltpu.VMEM(w_kv.shape, BF16),
            pltpu.VMEM(w_out.shape, BF16),
            pltpu.VMEM((block + LANES, cache.shape[2]), BF16),
            pltpu.VMEM((8, block + LANES), F32),
            pltpu.VMEM((rows, cols), F32),
            pltpu.VMEM((nq, n, 16, w1), BF16),
            pltpu.VMEM((nq, n, 16, w1), BF16),
            pltpu.VMEM((nq, 16, w2), BF16),
            pltpu.VMEM((nq, n, 16, w2), BF16),
            pltpu.VMEM((nu, n, 16, w3), BF16),
            pltpu.VMEM((nu, n, 16, w3), BF16),
            pltpu.VMEM((nu, n, 8, LANES), F32),
            pltpu.VMEM((nu, n, 8, LANES), F32),
            pltpu.VMEM((nu, 16, w3), BF16),
            pltpu.VMEM((nu, n, 16, w3), BF16),
            pltpu.VMEM((nch, rows, cw), BF16),
            pltpu.VMEM((nch, n, rows, cw), BF16),
            dma((2,)),
            dma((nq,)),
            dma((cfg["nc"],)),
            dma((nu,)),
            dma((nch,)),
        ]
        + [dma((nq, n))] * 4
        + [dma((nu, n))] * 6
        + [dma((nch, n))] * 2,
        compiler_params=pltpu.CompilerParams(
            collective_id=0, has_side_effects=True, vmem_limit_bytes=56 * 1024 * 1024
        ),
        cost_estimate=pl.CostEstimate(
            flops=2 * rows * feat * (qc + kc + cols) + 4 * 64 * block * 8 * 128,
            bytes_accessed=2 * (feat * (qc + kc) + w_out.size + cache.size),
            transcendentals=64 * 8 * block,
        ),
    )(
        perm, lengths, gain, inv,
        tokens.reshape(rows, feat), w_query, w_kv, w_out, cache,
    )
    return out.reshape(steps, req, cols)


def solution(mesh):
    n = mesh.shape["sect"]
    assert mesh.shape["tp"] == n
    return jax.shard_map(
        functools.partial(per_device, n),
        mesh=mesh,
        in_specs=(
            P(None, "groups", "tp"),
            P("tp"),
            P("tp", "sect"),
            P("tp", "sect"),
            P("sect", "tp"),
            P(("groups", "sect"), "tp", None),
            P(("groups", "sect"), None),
            P("groups"),
        ),
        out_specs=P(None, "groups", "tp"),
        check_vma=False,
    )
```

```python
import functools
import math

import jax
import jax.numpy as jnp
import numpy as np
from jax import lax
from jax.experimental import pallas as pl
from jax.experimental.pallas import tpu as pltpu
from jax.sharding import PartitionSpec as P

D = 8192
HEADS = 64
KV_HEADS = 8
HEAD_DIM = 128
PER_KV = HEADS // KV_HEADS
STEPS = 2
LANES = 128
MESH = pl.DeviceIdType.MESH
F32 = jnp.float32
BF16 = jnp.bfloat16


def pack(tiles):
    half = (len(tiles) + 1) // 2
    low = list(tiles[half:])
    if len(low) < half:
        low.append(jnp.zeros_like(tiles[0]))
    top = jnp.concatenate(tiles[:half], axis=1) if half > 1 else tiles[0]
    bottom = jnp.concatenate(low, axis=1) if half > 1 else low[0]
    return jnp.concatenate([top, bottom], axis=0).astype(BF16)


def unpack(packed, count):
    half = (count + 1) // 2
    wide = packed.astype(F32)
    return [
        wide[(i // half) * 8 : (i // half) * 8 + 8, (i % half) * LANES : (i % half + 1) * LANES]
        for i in range(count)
    ]


def kernel(
    cfg,
    perm_ref, len_ref, gain_ref, inv_ref, x_hbm, wq_hbm, wkv_hbm, wo_hbm, cache_hbm,
    out_hbm,
    x_v, wq_v, wkv_v, wo_v, kv_v, bias_v, fin_v, part_v,
    m1, r1, m2, r2, m3, r3, st, rst, m4, r4, m5, r5, m6,
    load_sem, wq_sem, cache_sem, wo_sem,
    s1, e1, s2, e2, s3, e3, s3b, e3b, s4, e4, s5, e5, s6, e6,
):
    n, rows, req, req_dev, block = cfg["n"], cfg["rows"], cfg["req"], cfg["req_dev"], cfg["block"]
    qc, kc, nq, unit, nu = cfg["qc"], cfg["kc"], cfg["nq"], cfg["unit"], cfg["nu"]
    half = cfg["half"]
    heads_per = HEADS // n
    total = block + LANES
    s = lax.axis_index("sect")
    t = lax.axis_index("tp")
    same = s == t

    def remote(src, dst, ssem, rsem, sect, tp):
        return pltpu.make_async_remote_copy(
            src_ref=src, dst_ref=dst, send_sem=ssem, recv_sem=rsem,
            device_id={"sect": sect, "tp": tp}, device_id_type=MESH,
        )

    x_copy = pltpu.make_async_copy(x_hbm, x_v, load_sem.at[0])
    x_copy.start()
    wkv_copy = pltpu.make_async_copy(wkv_hbm, wkv_v, load_sem.at[1])
    wkv_copy.start()
    qw = qc // nq
    wq_copies = [
        pltpu.make_async_copy(
            wq_hbm.at[:, pl.ds(i * qw, qw)], wq_v.at[:, pl.ds(i * qw, qw)], wq_sem.at[i]
        )
        for i in range(nq)
    ]
    for c in wq_copies:
        c.start()
    nc = cfg["nc"]
    crows = block // nc
    cache_copies = [
        pltpu.make_async_copy(
            cache_hbm.at[0, pl.ds(i * crows, crows)],
            kv_v.at[pl.ds(i * crows, crows)],
            cache_sem.at[i],
        )
        for i in range(nc)
    ]
    uw = unit * HEAD_DIM
    wo_copies = [
        pltpu.make_async_copy(wo_hbm.at[pl.ds(u * uw, uw)], wo_v.at[pl.ds(u * uw, uw)], wo_sem.at[u])
        for u in range(nu)
    ]

    barrier = pltpu.get_barrier_semaphore()
    for i in range(1, n):
        pl.semaphore_signal(
            barrier, inc=1, device_id={"sect": s, "tp": lax.rem(t + i, n)}, device_id_type=MESH
        )
        pl.semaphore_signal(
            barrier, inc=1, device_id={"sect": lax.rem(s + i, n), "tp": t}, device_id_type=MESH
        )
        pl.semaphore_signal(
            barrier, inc=1, device_id={"sect": lax.rem(s + i, n), "tp": s}, device_id_type=MESH
        )

    @pl.when(jnp.logical_not(same))
    def _():
        pl.semaphore_signal(barrier, inc=1, device_id={"sect": s, "tp": s}, device_id_type=MESH)

    ri = lax.broadcasted_iota(jnp.int32, (rows, rows), 0)
    ci = lax.broadcasted_iota(jnp.int32, (rows, rows), 1)
    big = 4096

    def slot_code(idx):
        return (idx >> 3) * req_dev + (idx & (req_dev - 1)) + ((idx & 7) >= req_dev).astype(jnp.int32) * big

    by_col = jnp.zeros((rows, rows), jnp.int32)
    by_row = jnp.zeros((rows, rows), jnp.int32)
    for c in range(rows):
        code = perm_ref[c % req] + (c // req) * big
        by_col = jnp.where(ci == c, code, by_col)
        by_row = jnp.where(ri == c, code, by_row)
    select = (by_col == slot_code(ri)).astype(F32).astype(BF16)
    select_back = (by_row == slot_code(ci)).astype(F32).astype(BF16)

    x_copy.wait()
    xs = jnp.dot(select, x_v[...], preferred_element_type=F32)
    square = jnp.sum(xs * xs, axis=1, keepdims=True)
    scaled = (xs * gain_ref[...].astype(F32).reshape(1, -1)).astype(BF16)

    r8 = lax.broadcasted_iota(jnp.int32, (8, LANES), 0)
    lane = lax.broadcasted_iota(jnp.int32, (8, LANES), 1)
    lens = [len_ref[0, j] for j in range(req_dev)]
    ends = []
    run = 0
    for j in range(req_dev):
        run = run + lens[j]
        ends.append(run)

    hi = square.astype(BF16).astype(F32)
    lo = square - hi
    lane_r = lax.broadcasted_iota(jnp.int32, (rows, LANES), 1)
    sq_tile = jnp.where(lane_r < 64, hi, lo)
    qt = qw // LANES
    kt = kc // LANES
    counts = [qt + (kt if h == 0 else 0) for h in range(nq)]
    w1 = [pl.ds(0, (counts[h] + (h == 0) + 1) // 2 * LANES) for h in range(nq)]
    w2 = [pl.ds(0, (counts[h] + 1) // 2 * LANES) for h in range(nq)]

    def tile_rows(array, o):
        return [
            array[o * 8 : o * 8 + 8, i * LANES : (i + 1) * LANES]
            for i in range(array.shape[1] // LANES)
        ]

    wkv_copy.wait()
    kpart = jnp.dot(scaled, wkv_v[...], preferred_element_type=F32)
    for h in range(nq):
        wq_copies[h].wait()
        if h == nq - 1:
            for c in cache_copies:
                c.start()
            for c in wo_copies:
                c.start()
        qpart = jnp.dot(scaled, wq_v[:, h * qw : (h + 1) * qw], preferred_element_type=F32)
        for o in range(n):
            tiles = tile_rows(qpart, o)
            if h == 0:
                tiles = tile_rows(kpart, o) + tiles + [sq_tile[o * 8 : o * 8 + 8]]
            m1[h, o, :, w1[h]] = pack(tiles)
        if h == 0:
            pl.semaphore_wait(barrier, 3 * (n - 1) + jnp.where(same, 0, 1))
        for i in range(1, n):
            to = lax.rem(t + i, n)
            remote(
                m1.at[h, to, :, w1[h]], r1.at[h, t, :, w1[h]], s1.at[h, i], e1.at[h, t], s, to
            ).start()

    pos = (r8 >= req_dev).astype(jnp.int32)
    step_row = pos
    for j in range(req_dev):
        pos = pos + jnp.where((r8 & (req_dev - 1)) == j, lens[j], 0)
    angle = pos.astype(F32) * inv_ref[...]
    cosine = jnp.cos(angle)
    sine = jnp.sin(angle)
    sine = jnp.where(lane < HEAD_DIM // 2, -sine, sine)
    rj = lax.broadcasted_iota(jnp.int32, (8, total), 0) & (req_dev - 1)
    rk = (lax.broadcasted_iota(jnp.int32, (8, total), 0) >= req_dev).astype(jnp.int32)
    col = lax.broadcasted_iota(jnp.int32, (8, total), 1)
    first = t * block
    low_b = jnp.zeros((8, total), jnp.int32)
    high_b = jnp.zeros((8, total), jnp.int32)
    for j in range(req_dev):
        low_b = jnp.where(rj == j, ends[j] - lens[j] - first, low_b)
        high_b = jnp.where(rj == j, ends[j] - first, high_b)
    old_ok = (col >= low_b) & (col < high_b) & (col < block)
    nidx = col - block
    new_limit = jnp.where(t == 0, block + 8, block)
    new_ok = (
        (col >= block) & (col < new_limit) & ((nidx & (req_dev - 1)) == rj)
        & ((nidx >= req_dev).astype(jnp.int32) <= rk)
    )
    bias_v[...] = jnp.where(old_ok | new_ok, 0.0, -1e30)
    kv_v[block + 16 : total, :] = jnp.zeros((LANES - 16, 2 * KV_HEADS * HEAD_DIM), BF16)

    inv_rms = None
    for h in range(nq):
        count = counts[h] + (h == 0)
        sums = unpack(m1[h, t, :, w1[h]], count)
        for i in range(1, n):
            src = lax.rem(t + i, n)
            remote(
                m1.at[h, src, :, w1[h]], r1.at[h, src, :, w1[h]], s1.at[h, i], e1.at[h, src], s, src
            ).wait_recv()
            sums = [a + b for a, b in zip(sums, unpack(r1[h, src, :, w1[h]], count))]
        if h == 0:
            sq = sums[-1][:, 0:1] + sums[-1][:, 64:65]
            inv_rms = lax.rsqrt(sq * (1.0 / D) + 1e-05)
            sums = sums[:-1]
        m2[h, :, w2[h]] = pack([a * inv_rms for a in sums])
        for i in range(1, n):
            to = lax.rem(t + i, n)
            remote(
                m2.at[h, :, w2[h]], r2.at[h, s, :, w2[h]], s2.at[h, i], e2.at[h, s], t, to
            ).start()

        @pl.when(jnp.logical_not(same))
        def _():
            remote(
                m2.at[h, :, w2[h]], r2.at[h, s, :, w2[h]], s2.at[h, 0], e2.at[h, s], t, t
            ).start()

        @pl.when(same)
        def _():
            r2[h, s, :, w2[h]] = m2[h, :, w2[h]]

    for c in cache_copies:
        c.wait()
    held = {}

    def routed(src, h):
        if (src, h) not in held:
            @pl.when(jnp.logical_not(same & (s == src)))
            def _():
                remote(
                    m2.at[h, :, w2[h]], r2.at[h, src, :, w2[h]], s2.at[h, 0], e2.at[h, src], t, t
                ).wait_recv()

            held[src, h] = unpack(r2[h, src, :, w2[h]], counts[h])
        return held[src, h]

    per_src = nq * qt

    def q_tile(head):
        src, inner = head // per_src, head % per_src
        return routed(src, inner // qt)[(kt if inner // qt == 0 else 0) + inner % qt]

    def kv_tile(index):
        return routed(index // kt, 0)[index % kt]

    def rotate(a):
        return a * cosine + pltpu.roll(a, HEAD_DIM // 2, 1) * sine

    def last_part(g):
        return max((head % per_src) // qt for head in range(g * PER_KV, (g + 1) * PER_KV))

    factor = math.log2(math.e) / math.sqrt(HEAD_DIM)
    zero8 = jnp.zeros((8, LANES), F32)
    for g in sorted(range(KV_HEADS), key=lambda g: (last_part(g), g)):
        kcol = slice(g * 256, g * 256 + 128)
        vcol = slice(g * 256 + 128, g * 256 + 256)
        kv_v[block : block + 16, kcol] = jnp.concatenate(
            [rotate(kv_tile(2 * g)), zero8], axis=0
        ).astype(BF16)
        kv_v[block : block + 16, vcol] = jnp.concatenate(
            [kv_tile(2 * g + 1), zero8], axis=0
        ).astype(BF16)
        q = jnp.concatenate(
            [rotate(q_tile(g * PER_KV + h)) for h in range(PER_KV)], axis=0
        ).astype(BF16)
        sc = lax.dot_general(
            q, kv_v[:, kcol], (((1,), (1,)), ((), ())), preferred_element_type=F32
        )
        sc = sc.reshape(PER_KV, 8, total) * factor + bias_v[...][None]
        top = jnp.maximum(jnp.max(sc, axis=2, keepdims=True), -1e20)
        w = jnp.exp2(sc - top)
        tot = jnp.sum(w, axis=2, keepdims=True)
        o = jnp.dot(
            w.reshape(PER_KV * 8, total).astype(BF16), kv_v[:, vcol],
            preferred_element_type=F32,
        )
        for first_head in range(0, PER_KV, unit):
            head = g * PER_KV + first_head
            d, u = head // heads_per, (head % heads_per) // unit
            hs = range(first_head, first_head + unit)
            m3[u, d] = pack([o[h * 8 : h * 8 + 8] for h in hs])
            stat = zero8
            for a, h in enumerate(hs):
                stat = jnp.where(lane == a, top[h], stat)
                stat = jnp.where(lane == 64 + a, tot[h], stat)
            st[u, d] = stat

            @pl.when(t != d)
            def _():
                remote(st.at[u, d], rst.at[u, t], s3b.at[u, d], e3b.at[u, t], s, d).start()
                remote(m3.at[u, d], r3.at[u, t], s3.at[u, d], e3.at[u, t], s, d).start()

    for u in range(nu):
        stats = [st[u, t]]
        for i in range(1, n):
            src = lax.rem(t + i, n)
            remote(
                st.at[u, src], rst.at[u, src], s3b.at[u, src], e3b.at[u, src], s, src
            ).wait_recv()
            stats.append(rst[u, src])
        best = functools.reduce(jnp.maximum, stats)
        decay = [jnp.exp2(jnp.minimum(a - best, 0.0)) for a in stats]
        norm = sum(f * pltpu.roll(a, 64, 1) for f, a in zip(decay, stats))
        share = [f / norm for f in decay]
        att = [a * share[0][:, i : i + 1] for i, a in enumerate(unpack(m3[u, t], unit))]
        for i in range(1, n):
            src = lax.rem(t + i, n)
            remote(m3.at[u, src], r3.at[u, src], s3.at[u, src], e3.at[u, src], s, src).wait_recv()
            att = [
                a + b * share[i][:, k : k + 1]
                for k, (a, b) in enumerate(zip(att, unpack(r3[u, src], unit)))
            ]
        m4[u] = pack(att)
        for i in range(1, n):
            to = lax.rem(t + i, n)
            remote(m4.at[u], r4.at[u, s], s4.at[u, i], e4.at[u, s], t, to).start()

        @pl.when(jnp.logical_not(same))
        def _():
            remote(m4.at[u], r4.at[u, s], s4.at[u, 0], e4.at[u, s], t, t).start()

        @pl.when(same)
        def _():
            r4[u, s] = m4[u]

    lefts = []
    for u in range(nu):
        for src in range(n):
            @pl.when(jnp.logical_not(same & (s == src)))
            def _():
                remote(m4.at[u], r4.at[u, src], s4.at[u, 0], e4.at[u, src], t, t).wait_recv()

        attended = jnp.concatenate(
            [jnp.concatenate(unpack(r4[u, src], unit), axis=1) for src in range(n)], axis=0
        ).astype(BF16)
        lefts.append(jnp.dot(select_back, attended, preferred_element_type=F32).astype(BF16))
        wo_copies[u].wait()
        if u < nu - 1:
            early = jnp.dot(lefts[u], wo_v[u * uw : (u + 1) * uw, :], preferred_element_type=F32)
            fin_v[...] = early if u == 0 else fin_v[...] + early

    core = lax.rem(s, 2)
    partner = s + 1 - 2 * core
    u = nu - 1
    for c in range(2):
        ccol = slice(c * half, (c + 1) * half)
        part = jnp.dot(lefts[u], wo_v[u * uw : (u + 1) * uw, ccol], preferred_element_type=F32)
        if nu > 1:
            part = part + fin_v[:, ccol]
        part_v[c] = part

        @pl.when(core != c)
        def _():
            m5[...] = part.astype(BF16)
            remote(m5, r5, s5.at[0], e5.at[0], partner, t).start()

    remote(m5, r5, s5.at[0], e5.at[0], partner, t).wait_recv()
    m6[...] = (part_v[core] + r5[...].astype(F32)).astype(BF16)

    def landing(src):
        return out_hbm.at[
            src // 2, :, pl.ds(pl.multiple_of(lax.rem(src, 2) * half, half), half)
        ]

    order = sorted(range(1, n), key=lambda i: i % 2)
    for i in order:
        remote(m6, landing(s), s6.at[i], e6.at[s], lax.rem(s + i, n), t).start()
    own = pltpu.make_async_copy(m6, landing(s), load_sem.at[2])
    own.start()

    for i in range(1, n):
        to = lax.rem(t + i, n)
        for h in range(nq):
            remote(
                m1.at[h, to, :, w1[h]], r1.at[h, t, :, w1[h]], s1.at[h, i], e1.at[h, t], s, to
            ).wait_send()
            remote(
                m2.at[h, :, w2[h]], r2.at[h, s, :, w2[h]], s2.at[h, i], e2.at[h, s], t, to
            ).wait_send()
        for u in range(nu):
            remote(m4.at[u], r4.at[u, s], s4.at[u, i], e4.at[u, s], t, to).wait_send()
            remote(m3.at[u, to], r3.at[u, t], s3.at[u, to], e3.at[u, t], s, to).wait_send()
            remote(st.at[u, to], rst.at[u, t], s3b.at[u, to], e3b.at[u, t], s, to).wait_send()

    @pl.when(jnp.logical_not(same))
    def _():
        for h in range(nq):
            remote(
                m2.at[h, :, w2[h]], r2.at[h, s, :, w2[h]], s2.at[h, 0], e2.at[h, s], t, t
            ).wait_send()
        for u in range(nu):
            remote(m4.at[u], r4.at[u, s], s4.at[u, 0], e4.at[u, s], t, t).wait_send()

    remote(m5, r5, s5.at[0], e5.at[0], partner, t).wait_send()
    own.wait()
    for i in order:
        src = lax.rem(s + i, n)
        remote(m6, landing(s), s6.at[i], e6.at[s], src, t).wait_send()
        remote(m6, landing(src), s6.at[i], e6.at[src], src, t).wait_recv()


def per_device(n, tokens, gain, w_query, w_kv, w_out, cache, lengths, perm):
    steps, req, feat = tokens.shape
    rows = steps * req
    req_dev = lengths.shape[1]
    block = cache.shape[1]
    qc, kc = w_query.shape[1], w_kv.shape[1]
    cols = w_out.shape[1]
    heads_per = HEADS // n
    unit = min(heads_per, PER_KV)
    nu = heads_per // unit
    nq = max(1, qc // 1024)
    half = cols // 2
    assert n % 2 == 0
    assert steps == STEPS and steps * req_dev == 8 and req == n * req_dev
    cfg = dict(
        n=n, rows=rows, req=req, req_dev=req_dev, block=block, qc=qc, kc=kc,
        nq=nq, nc=4, unit=unit, nu=nu, half=half,
    )
    widest = qc // nq // LANES + kc // LANES
    w1 = (widest + 2) // 2 * LANES
    w2 = (widest + 1) // 2 * LANES
    w3 = (unit + 1) // 2 * LANES
    inv = np.exp(-(2.0 * np.arange(64) / HEAD_DIM) * math.log(500000.0)).astype(np.float32)
    inv = jnp.asarray(np.concatenate([inv, inv])[None])
    any_spec = pl.BlockSpec(memory_space=pl.ANY)
    smem = pl.BlockSpec(memory_space=pltpu.SMEM)
    vmem = pl.BlockSpec(memory_space=pltpu.VMEM)
    dma = pltpu.SemaphoreType.DMA
    sums = pl.pallas_call(
        functools.partial(kernel, cfg),
        out_shape=jax.ShapeDtypeStruct((n // 2, rows, cols), BF16),
        in_specs=[smem, smem, vmem, vmem] + [any_spec] * 5,
        out_specs=any_spec,
        scratch_shapes=[
            pltpu.VMEM((rows, feat), BF16),
            pltpu.VMEM(w_query.shape, BF16),
            pltpu.VMEM(w_kv.shape, BF16),
            pltpu.VMEM(w_out.shape, BF16),
            pltpu.VMEM((block + LANES, cache.shape[2]), BF16),
            pltpu.VMEM((8, block + LANES), F32),
            pltpu.VMEM((rows, cols), F32),
            pltpu.VMEM((2, rows, half), F32),
            pltpu.VMEM((nq, n, 16, w1), BF16),
            pltpu.VMEM((nq, n, 16, w1), BF16),
            pltpu.VMEM((nq, 16, w2), BF16),
            pltpu.VMEM((nq, n, 16, w2), BF16),
            pltpu.VMEM((nu, n, 16, w3), BF16),
            pltpu.VMEM((nu, n, 16, w3), BF16),
            pltpu.VMEM((nu, n, 8, LANES), F32),
            pltpu.VMEM((nu, n, 8, LANES), F32),
            pltpu.VMEM((nu, 16, w3), BF16),
            pltpu.VMEM((nu, n, 16, w3), BF16),
            pltpu.VMEM((rows, half), BF16),
            pltpu.VMEM((rows, half), BF16),
            pltpu.VMEM((rows, half), BF16),
            dma((3,)),
            dma((nq,)),
            dma((cfg["nc"],)),
            dma((nu,)),
        ]
        + [dma((nq, n))] * 4
        + [dma((nu, n))] * 6
        + [dma((1,))] * 2
        + [dma((n,))] * 2,
        compiler_params=pltpu.CompilerParams(
            collective_id=0, has_side_effects=True, vmem_limit_bytes=56 * 1024 * 1024
        ),
        cost_estimate=pl.CostEstimate(
            flops=2 * rows * feat * (qc + kc + cols) + 4 * 64 * block * 8 * 128,
            bytes_accessed=2 * (feat * (qc + kc) + w_out.size + cache.size),
            transcendentals=64 * 8 * block,
        ),
    )(
        perm, lengths, gain, inv,
        tokens.reshape(rows, feat), w_query, w_kv, w_out, cache,
    )
    summed = functools.reduce(jnp.add, [sums[c].astype(F32) for c in range(n // 2)])
    return (tokens.astype(F32) + summed.reshape(steps, req, cols)).astype(BF16)


def solution(mesh):
    n = mesh.shape["sect"]
    assert mesh.shape["tp"] == n
    return jax.shard_map(
        functools.partial(per_device, n),
        mesh=mesh,
        in_specs=(
            P(None, "groups", "tp"),
            P("tp"),
            P("tp", "sect"),
            P("tp", "sect"),
            P("sect", "tp"),
            P(("groups", "sect"), "tp", None),
            P(("groups", "sect"), None),
            P("groups"),
        ),
        out_specs=P(None, "groups", "tp"),
        check_vma=False,
    )
```

```python
import functools
import math

import jax
import jax.numpy as jnp
import numpy as np
from jax import lax
from jax.experimental import pallas as pl
from jax.experimental.pallas import tpu as pltpu
from jax.sharding import PartitionSpec as P

D = 8192
HEADS = 64
KV_HEADS = 8
HEAD_DIM = 128
PER_KV = HEADS // KV_HEADS
STEPS = 2
LANES = 128
MESH = pl.DeviceIdType.MESH
F32 = jnp.float32
BF16 = jnp.bfloat16


def pack(tiles):
    half = (len(tiles) + 1) // 2
    low = list(tiles[half:])
    if len(low) < half:
        low.append(jnp.zeros_like(tiles[0]))
    top = jnp.concatenate(tiles[:half], axis=1) if half > 1 else tiles[0]
    bottom = jnp.concatenate(low, axis=1) if half > 1 else low[0]
    return jnp.concatenate([top, bottom], axis=0).astype(BF16)


def unpack(packed, count):
    half = (count + 1) // 2
    wide = packed.astype(F32)
    return [
        wide[(i // half) * 8 : (i // half) * 8 + 8, (i % half) * LANES : (i % half + 1) * LANES]
        for i in range(count)
    ]


def kernel(
    cfg,
    perm_ref, len_ref, gain_ref, inv_ref, x_hbm, wq_hbm, wkv_hbm, wo_hbm, cache_hbm,
    out_hbm,
    x_v, wq_v, wkv_v, wo_v, kv_v, bias_v, fin_v,
    m1, r1, m2, r2, m3, r3, st, rst, m4, r4, m5, r5, m6,
    load_sem, wq_sem, cache_sem, wo_sem,
    s1, e1, s2, e2, s3, e3, s3b, e3b, s4, e4, s5, e5, s6, e6,
):
    n, rows, req, req_dev, block = cfg["n"], cfg["rows"], cfg["req"], cfg["req_dev"], cfg["block"]
    qc, kc, nq, unit, nu = cfg["qc"], cfg["kc"], cfg["nq"], cfg["unit"], cfg["nu"]
    half = cfg["half"]
    heads_per = HEADS // n
    total = block + LANES
    s = lax.axis_index("sect")
    t = lax.axis_index("tp")
    same = s == t

    def remote(src, dst, ssem, rsem, sect, tp):
        return pltpu.make_async_remote_copy(
            src_ref=src, dst_ref=dst, send_sem=ssem, recv_sem=rsem,
            device_id={"sect": sect, "tp": tp}, device_id_type=MESH,
        )

    x_copy = pltpu.make_async_copy(x_hbm, x_v, load_sem.at[0])
    x_copy.start()
    wkv_copy = pltpu.make_async_copy(wkv_hbm, wkv_v, load_sem.at[1])
    wkv_copy.start()
    qw = qc // nq
    wq_copies = [
        pltpu.make_async_copy(
            wq_hbm.at[:, pl.ds(i * qw, qw)], wq_v.at[:, pl.ds(i * qw, qw)], wq_sem.at[i]
        )
        for i in range(nq)
    ]
    for c in wq_copies:
        c.start()
    nc = cfg["nc"]
    crows = block // nc
    cache_copies = [
        pltpu.make_async_copy(
            cache_hbm.at[0, pl.ds(i * crows, crows)],
            kv_v.at[pl.ds(i * crows, crows)],
            cache_sem.at[i],
        )
        for i in range(nc)
    ]
    uw = unit * HEAD_DIM
    wo_copies = [
        pltpu.make_async_copy(wo_hbm.at[pl.ds(u * uw, uw)], wo_v.at[pl.ds(u * uw, uw)], wo_sem.at[u])
        for u in range(nu)
    ]

    barrier = pltpu.get_barrier_semaphore()
    for i in range(1, n):
        pl.semaphore_signal(
            barrier, inc=1, device_id={"sect": s, "tp": lax.rem(t + i, n)}, device_id_type=MESH
        )
        pl.semaphore_signal(
            barrier, inc=1, device_id={"sect": lax.rem(s + i, n), "tp": t}, device_id_type=MESH
        )
        pl.semaphore_signal(
            barrier, inc=1, device_id={"sect": lax.rem(s + i, n), "tp": s}, device_id_type=MESH
        )

    @pl.when(jnp.logical_not(same))
    def _():
        pl.semaphore_signal(barrier, inc=1, device_id={"sect": s, "tp": s}, device_id_type=MESH)

    ri = lax.broadcasted_iota(jnp.int32, (rows, rows), 0)
    ci = lax.broadcasted_iota(jnp.int32, (rows, rows), 1)
    big = 4096

    def slot_code(idx):
        return (idx >> 3) * req_dev + (idx & (req_dev - 1)) + ((idx & 7) >= req_dev).astype(jnp.int32) * big

    by_col = jnp.zeros((rows, rows), jnp.int32)
    by_row = jnp.zeros((rows, rows), jnp.int32)
    for c in range(rows):
        code = perm_ref[c % req] + (c // req) * big
        by_col = jnp.where(ci == c, code, by_col)
        by_row = jnp.where(ri == c, code, by_row)
    select = (by_col == slot_code(ri)).astype(F32).astype(BF16)
    select_back = (by_row == slot_code(ci)).astype(F32).astype(BF16)

    x_copy.wait()
    xs = jnp.dot(select, x_v[...], preferred_element_type=F32)
    square = jnp.sum(xs * xs, axis=1, keepdims=True)
    scaled = (xs * gain_ref[...].astype(F32).reshape(1, -1)).astype(BF16)

    r8 = lax.broadcasted_iota(jnp.int32, (8, LANES), 0)
    lane = lax.broadcasted_iota(jnp.int32, (8, LANES), 1)
    lens = [len_ref[0, j] for j in range(req_dev)]
    ends = []
    run = 0
    for j in range(req_dev):
        run = run + lens[j]
        ends.append(run)

    hi = square.astype(BF16).astype(F32)
    lo = square - hi
    lane_r = lax.broadcasted_iota(jnp.int32, (rows, LANES), 1)
    sq_tile = jnp.where(lane_r < 64, hi, lo)
    qt = qw // LANES
    kt = kc // LANES
    counts = [qt + (kt if h == 0 else 0) for h in range(nq)]
    w1 = [pl.ds(0, (counts[h] + (h == 0) + 1) // 2 * LANES) for h in range(nq)]
    w2 = [pl.ds(0, (counts[h] + 1) // 2 * LANES) for h in range(nq)]

    def tile_rows(array, o):
        return [
            array[o * 8 : o * 8 + 8, i * LANES : (i + 1) * LANES]
            for i in range(array.shape[1] // LANES)
        ]

    wkv_copy.wait()
    kpart = jnp.dot(scaled, wkv_v[...], preferred_element_type=F32)
    for h in range(nq):
        wq_copies[h].wait()
        if h == nq - 1:
            for c in cache_copies:
                c.start()
            for c in wo_copies:
                c.start()
        qpart = jnp.dot(scaled, wq_v[:, h * qw : (h + 1) * qw], preferred_element_type=F32)
        for o in range(n):
            tiles = tile_rows(qpart, o)
            if h == 0:
                tiles = tile_rows(kpart, o) + tiles + [sq_tile[o * 8 : o * 8 + 8]]
            m1[h, o, :, w1[h]] = pack(tiles)
        if h == 0:
            pl.semaphore_wait(barrier, 3 * (n - 1) + jnp.where(same, 0, 1))
        for i in range(1, n):
            to = lax.rem(t + i, n)
            remote(
                m1.at[h, to, :, w1[h]], r1.at[h, t, :, w1[h]], s1.at[h, i], e1.at[h, t], s, to
            ).start()

    pos = (r8 >= req_dev).astype(jnp.int32)
    step_row = pos
    for j in range(req_dev):
        pos = pos + jnp.where((r8 & (req_dev - 1)) == j, lens[j], 0)
    angle = pos.astype(F32) * inv_ref[...]
    cosine = jnp.cos(angle)
    sine = jnp.sin(angle)
    sine = jnp.where(lane < HEAD_DIM // 2, -sine, sine)
    rj = lax.broadcasted_iota(jnp.int32, (8, total), 0) & (req_dev - 1)
    rk = (lax.broadcasted_iota(jnp.int32, (8, total), 0) >= req_dev).astype(jnp.int32)
    col = lax.broadcasted_iota(jnp.int32, (8, total), 1)
    first = t * block
    low_b = jnp.zeros((8, total), jnp.int32)
    high_b = jnp.zeros((8, total), jnp.int32)
    for j in range(req_dev):
        low_b = jnp.where(rj == j, ends[j] - lens[j] - first, low_b)
        high_b = jnp.where(rj == j, ends[j] - first, high_b)
    old_ok = (col >= low_b) & (col < high_b) & (col < block)
    nidx = col - block
    new_limit = jnp.where(t == 0, block + 8, block)
    new_ok = (
        (col >= block) & (col < new_limit) & ((nidx & (req_dev - 1)) == rj)
        & ((nidx >= req_dev).astype(jnp.int32) <= rk)
    )
    bias_v[...] = jnp.where(old_ok | new_ok, 0.0, -1e30)
    kv_v[block + 16 : total, :] = jnp.zeros((LANES - 16, 2 * KV_HEADS * HEAD_DIM), BF16)

    inv_rms = None
    for h in range(nq):
        count = counts[h] + (h == 0)
        sums = unpack(m1[h, t, :, w1[h]], count)
        for i in range(1, n):
            src = lax.rem(t + i, n)
            remote(
                m1.at[h, src, :, w1[h]], r1.at[h, src, :, w1[h]], s1.at[h, i], e1.at[h, src], s, src
            ).wait_recv()
            sums = [a + b for a, b in zip(sums, unpack(r1[h, src, :, w1[h]], count))]
        if h == 0:
            sq = sums[-1][:, 0:1] + sums[-1][:, 64:65]
            inv_rms = lax.rsqrt(sq * (1.0 / D) + 1e-05)
            sums = sums[:-1]
        m2[h, :, w2[h]] = pack([a * inv_rms for a in sums])
        for i in range(1, n):
            to = lax.rem(t + i, n)
            remote(
                m2.at[h, :, w2[h]], r2.at[h, s, :, w2[h]], s2.at[h, i], e2.at[h, s], t, to
            ).start()

        @pl.when(jnp.logical_not(same))
        def _():
            remote(
                m2.at[h, :, w2[h]], r2.at[h, s, :, w2[h]], s2.at[h, 0], e2.at[h, s], t, t
            ).start()

        @pl.when(same)
        def _():
            r2[h, s, :, w2[h]] = m2[h, :, w2[h]]

    for c in cache_copies:
        c.wait()
    held = {}

    def routed(src, h):
        if (src, h) not in held:
            @pl.when(jnp.logical_not(same & (s == src)))
            def _():
                remote(
                    m2.at[h, :, w2[h]], r2.at[h, src, :, w2[h]], s2.at[h, 0], e2.at[h, src], t, t
                ).wait_recv()

            held[src, h] = unpack(r2[h, src, :, w2[h]], counts[h])
        return held[src, h]

    per_src = nq * qt

    def q_tile(head):
        src, inner = head // per_src, head % per_src
        return routed(src, inner // qt)[(kt if inner // qt == 0 else 0) + inner % qt]

    def kv_tile(index):
        return routed(index // kt, 0)[index % kt]

    def rotate(a):
        return a * cosine + pltpu.roll(a, HEAD_DIM // 2, 1) * sine

    def last_part(g):
        return max((head % per_src) // qt for head in range(g * PER_KV, (g + 1) * PER_KV))

    factor = math.log2(math.e) / math.sqrt(HEAD_DIM)
    zero8 = jnp.zeros((8, LANES), F32)
    for g in sorted(range(KV_HEADS), key=lambda g: (last_part(g), g)):
        kcol = slice(g * 256, g * 256 + 128)
        vcol = slice(g * 256 + 128, g * 256 + 256)
        kv_v[block : block + 16, kcol] = jnp.concatenate(
            [rotate(kv_tile(2 * g)), zero8], axis=0
        ).astype(BF16)
        kv_v[block : block + 16, vcol] = jnp.concatenate(
            [kv_tile(2 * g + 1), zero8], axis=0
        ).astype(BF16)
        q = jnp.concatenate(
            [rotate(q_tile(g * PER_KV + h)) for h in range(PER_KV)], axis=0
        ).astype(BF16)
        sc = lax.dot_general(
            q, kv_v[:, kcol], (((1,), (1,)), ((), ())), preferred_element_type=F32
        )
        sc = sc.reshape(PER_KV, 8, total) * factor + bias_v[...][None]
        top = jnp.maximum(jnp.max(sc, axis=2, keepdims=True), -1e20)
        w = jnp.exp2(sc - top)
        tot = jnp.sum(w, axis=2, keepdims=True)
        o = jnp.dot(
            w.reshape(PER_KV * 8, total).astype(BF16), kv_v[:, vcol],
            preferred_element_type=F32,
        )
        for first_head in range(0, PER_KV, unit):
            head = g * PER_KV + first_head
            d, u = head // heads_per, (head % heads_per) // unit
            hs = range(first_head, first_head + unit)
            m3[u, d] = pack([o[h * 8 : h * 8 + 8] for h in hs])
            stat = zero8
            for a, h in enumerate(hs):
                stat = jnp.where(lane == a, top[h], stat)
                stat = jnp.where(lane == 64 + a, tot[h], stat)
            st[u, d] = stat

            @pl.when(t != d)
            def _():
                remote(st.at[u, d], rst.at[u, t], s3b.at[u, d], e3b.at[u, t], s, d).start()
                remote(m3.at[u, d], r3.at[u, t], s3.at[u, d], e3.at[u, t], s, d).start()

    for u in range(nu):
        stats = [st[u, t]]
        for i in range(1, n):
            src = lax.rem(t + i, n)
            remote(
                st.at[u, src], rst.at[u, src], s3b.at[u, src], e3b.at[u, src], s, src
            ).wait_recv()
            stats.append(rst[u, src])
        best = functools.reduce(jnp.maximum, stats)
        decay = [jnp.exp2(jnp.minimum(a - best, 0.0)) for a in stats]
        norm = sum(f * pltpu.roll(a, 64, 1) for f, a in zip(decay, stats))
        share = [f / norm for f in decay]
        att = [a * share[0][:, i : i + 1] for i, a in enumerate(unpack(m3[u, t], unit))]
        for i in range(1, n):
            src = lax.rem(t + i, n)
            remote(m3.at[u, src], r3.at[u, src], s3.at[u, src], e3.at[u, src], s, src).wait_recv()
            att = [
                a + b * share[i][:, k : k + 1]
                for k, (a, b) in enumerate(zip(att, unpack(r3[u, src], unit)))
            ]
        m4[u] = pack(att)
        for i in range(1, n):
            to = lax.rem(t + i, n)
            remote(m4.at[u], r4.at[u, s], s4.at[u, i], e4.at[u, s], t, to).start()

        @pl.when(jnp.logical_not(same))
        def _():
            remote(m4.at[u], r4.at[u, s], s4.at[u, 0], e4.at[u, s], t, t).start()

        @pl.when(same)
        def _():
            r4[u, s] = m4[u]

    lefts = []
    for u in range(nu):
        for src in range(n):
            @pl.when(jnp.logical_not(same & (s == src)))
            def _():
                remote(m4.at[u], r4.at[u, src], s4.at[u, 0], e4.at[u, src], t, t).wait_recv()

        attended = jnp.concatenate(
            [jnp.concatenate(unpack(r4[u, src], unit), axis=1) for src in range(n)], axis=0
        ).astype(BF16)
        lefts.append(jnp.dot(select_back, attended, preferred_element_type=F32).astype(BF16))
        wo_copies[u].wait()
        if u < nu - 1:
            early = jnp.dot(lefts[u], wo_v[u * uw : (u + 1) * uw, :], preferred_element_type=F32)
            fin_v[...] = early if u == 0 else fin_v[...] + early

    core = lax.rem(s, 2)
    partner = s + 1 - 2 * core
    u = nu - 1
    def half_sum(c):
        ccol = pl.ds(pl.multiple_of(c * half, half), half)
        part = jnp.dot(lefts[u], wo_v[u * uw : (u + 1) * uw, ccol], preferred_element_type=F32)
        return part + fin_v[:, ccol] if nu > 1 else part

    m5[...] = half_sum(1 - core).astype(BF16)
    remote(m5, r5, s5.at[0], e5.at[0], partner, t).start()
    kept = half_sum(core)
    remote(m5, r5, s5.at[0], e5.at[0], partner, t).wait_recv()
    m6[...] = (kept + r5[...].astype(F32)).astype(BF16)

    def landing(src):
        return out_hbm.at[
            src // 2, :, pl.ds(pl.multiple_of(lax.rem(src, 2) * half, half), half)
        ]

    order = sorted(range(1, n), key=lambda i: i % 2)
    for i in order:
        remote(m6, landing(s), s6.at[i], e6.at[s], lax.rem(s + i, n), t).start()
    own = pltpu.make_async_copy(m6, landing(s), load_sem.at[2])
    own.start()

    for i in range(1, n):
        to = lax.rem(t + i, n)
        for h in range(nq):
            remote(
                m1.at[h, to, :, w1[h]], r1.at[h, t, :, w1[h]], s1.at[h, i], e1.at[h, t], s, to
            ).wait_send()
            remote(
                m2.at[h, :, w2[h]], r2.at[h, s, :, w2[h]], s2.at[h, i], e2.at[h, s], t, to
            ).wait_send()
        for u in range(nu):
            remote(m4.at[u], r4.at[u, s], s4.at[u, i], e4.at[u, s], t, to).wait_send()
            remote(m3.at[u, to], r3.at[u, t], s3.at[u, to], e3.at[u, t], s, to).wait_send()
            remote(st.at[u, to], rst.at[u, t], s3b.at[u, to], e3b.at[u, t], s, to).wait_send()

    @pl.when(jnp.logical_not(same))
    def _():
        for h in range(nq):
            remote(
                m2.at[h, :, w2[h]], r2.at[h, s, :, w2[h]], s2.at[h, 0], e2.at[h, s], t, t
            ).wait_send()
        for u in range(nu):
            remote(m4.at[u], r4.at[u, s], s4.at[u, 0], e4.at[u, s], t, t).wait_send()

    remote(m5, r5, s5.at[0], e5.at[0], partner, t).wait_send()
    own.wait()
    for i in order:
        src = lax.rem(s + i, n)
        remote(m6, landing(s), s6.at[i], e6.at[s], src, t).wait_send()
        remote(m6, landing(src), s6.at[i], e6.at[src], src, t).wait_recv()


def per_device(n, tokens, gain, w_query, w_kv, w_out, cache, lengths, perm):
    steps, req, feat = tokens.shape
    rows = steps * req
    req_dev = lengths.shape[1]
    block = cache.shape[1]
    qc, kc = w_query.shape[1], w_kv.shape[1]
    cols = w_out.shape[1]
    heads_per = HEADS // n
    unit = min(heads_per, PER_KV)
    nu = heads_per // unit
    nq = max(1, qc // 1024)
    half = cols // 2
    assert n % 2 == 0
    assert steps == STEPS and steps * req_dev == 8 and req == n * req_dev
    cfg = dict(
        n=n, rows=rows, req=req, req_dev=req_dev, block=block, qc=qc, kc=kc,
        nq=nq, nc=4, unit=unit, nu=nu, half=half,
    )
    widest = qc // nq // LANES + kc // LANES
    w1 = (widest + 2) // 2 * LANES
    w2 = (widest + 1) // 2 * LANES
    w3 = (unit + 1) // 2 * LANES
    inv = np.exp(-(2.0 * np.arange(64) / HEAD_DIM) * math.log(500000.0)).astype(np.float32)
    inv = jnp.asarray(np.concatenate([inv, inv])[None])
    any_spec = pl.BlockSpec(memory_space=pl.ANY)
    smem = pl.BlockSpec(memory_space=pltpu.SMEM)
    vmem = pl.BlockSpec(memory_space=pltpu.VMEM)
    dma = pltpu.SemaphoreType.DMA
    sums = pl.pallas_call(
        functools.partial(kernel, cfg),
        out_shape=jax.ShapeDtypeStruct((n // 2, rows, cols), BF16),
        in_specs=[smem, smem, vmem, vmem] + [any_spec] * 5,
        out_specs=any_spec,
        scratch_shapes=[
            pltpu.VMEM((rows, feat), BF16),
            pltpu.VMEM(w_query.shape, BF16),
            pltpu.VMEM(w_kv.shape, BF16),
            pltpu.VMEM(w_out.shape, BF16),
            pltpu.VMEM((block + LANES, cache.shape[2]), BF16),
            pltpu.VMEM((8, block + LANES), F32),
            pltpu.VMEM((rows, cols), F32),
            pltpu.VMEM((nq, n, 16, w1), BF16),
            pltpu.VMEM((nq, n, 16, w1), BF16),
            pltpu.VMEM((nq, 16, w2), BF16),
            pltpu.VMEM((nq, n, 16, w2), BF16),
            pltpu.VMEM((nu, n, 16, w3), BF16),
            pltpu.VMEM((nu, n, 16, w3), BF16),
            pltpu.VMEM((nu, n, 8, LANES), F32),
            pltpu.VMEM((nu, n, 8, LANES), F32),
            pltpu.VMEM((nu, 16, w3), BF16),
            pltpu.VMEM((nu, n, 16, w3), BF16),
            pltpu.VMEM((rows, half), BF16),
            pltpu.VMEM((rows, half), BF16),
            pltpu.VMEM((rows, half), BF16),
            dma((3,)),
            dma((nq,)),
            dma((cfg["nc"],)),
            dma((nu,)),
        ]
        + [dma((nq, n))] * 4
        + [dma((nu, n))] * 6
        + [dma((1,))] * 2
        + [dma((n,))] * 2,
        compiler_params=pltpu.CompilerParams(
            collective_id=0, has_side_effects=True, vmem_limit_bytes=56 * 1024 * 1024
        ),
        cost_estimate=pl.CostEstimate(
            flops=2 * rows * feat * (qc + kc + cols) + 4 * 64 * block * 8 * 128,
            bytes_accessed=2 * (feat * (qc + kc) + w_out.size + cache.size),
            transcendentals=64 * 8 * block,
        ),
    )(
        perm, lengths, gain, inv,
        tokens.reshape(rows, feat), w_query, w_kv, w_out, cache,
    )
    summed = functools.reduce(jnp.add, [sums[c].astype(F32) for c in range(n // 2)])
    return (tokens.astype(F32) + summed.reshape(steps, req, cols)).astype(BF16)


def solution(mesh):
    n = mesh.shape["sect"]
    assert mesh.shape["tp"] == n
    return jax.shard_map(
        functools.partial(per_device, n),
        mesh=mesh,
        in_specs=(
            P(None, "groups", "tp"),
            P("tp"),
            P("tp", "sect"),
            P("tp", "sect"),
            P("sect", "tp"),
            P(("groups", "sect"), "tp", None),
            P(("groups", "sect"), None),
            P("groups"),
        ),
        out_specs=P(None, "groups", "tp"),
        check_vma=False,
    )
```
